512 devices in a mesh: dp: 32 (over z_lo, x), mp: 16 (over z_hi, y, core).
Axes of the slice: x: 4, y: 4, z: 16 (z_hi: 2, z_lo: 8; z = z_hi * 8 + z_lo), core: 2. Of those that a mesh axis runs over, the one named last changes fastest.
Arguments:
- teacher_in: bfloat16 [2048, 16384], P('dp', 'mp'), may hold values from -6 to 6
- teacher_weight: bfloat16 [16384, 8192], P('mp', 'dp'), may hold values from -0.046875 to 0.046875
- student_in: bfloat16 [2048, 8192], P('dp', 'mp'), may hold values from -6 to 6
- projection: bfloat16 [8192, 8192], P('mp', 'dp'), may hold values from -0.0625 to 0.0625
- owner_order: int32 [2048], P('mp'), may hold values from 0 to 127, as said below
Outputs:
- projection_grad: float32 [8192, 8192], P('mp', 'dp')
- cosine: float32 [2048], P('mp')
The draws below stay inside these ranges and needn't reach their ends.
Inputs may be any that keep to these rules, and one draw needn't show every extreme that they name: `owner_order`: each aligned block of 128 entries is a permutation of 0 to 127.
All inputs are finite; a program needn't handle non-finite values.
Results may differ from the reference program's by a relative error of at most 0.025.
Values may be sent and summed in bfloat16 or wider, within the bound.
No kernel may reach another device: no remote copies, remote signals or barrier semaphores. Data moves between devices by JAX's collectives and lax.ppermute only.
A program may use at most 64 MiB of HBM per device.

```python
import jax
import jax.numpy as jnp
from jax import lax

DT = 16384
DS = 8192
DTO = 8192
TOKENS = 2048
N_MP = 16


def draw_owner_order(key, part):
    key = jax.random.fold_in(key, 7)
    block_keys = jax.random.split(key, N_MP)
    orders = jax.vmap(lambda single: jax.random.permutation(single, TOKENS // N_MP))(block_keys)
    return orders.reshape(-1).astype(jnp.int32)


def block_levels(own_key, dims, shards, smallest, high):
    level = 1.0
    for dim, parts in shards:
        heights = jax.random.uniform(jax.random.fold_in(jax.random.fold_in(own_key, 6), dim), (parts,), jnp.float32, smallest / len(shards), high / len(shards))
        level = level * jnp.repeat(jnp.exp(heights), dims[dim] // parts).reshape((-1,) + (1,) * (len(dims) - 1 - dim))
    return level


def gaussian(stream_key, dims, scale, bound, cuts=(), kind=jnp.bfloat16):
    values = jax.random.normal(stream_key, dims, jnp.float32) * scale
    if len(cuts) > 0:
        values = block_levels(stream_key, dims, cuts, -0.22, 0.18) * values
    return jnp.clip(values, min=-bound, max=bound).astype(kind)


def setup_inputs(seed: int = 0) -> dict:
    streams_of = jax.random.split(jax.random.key(seed), 6)
    teacher_in = gaussian(streams_of[0], (TOKENS, DT), 1.0, 6.0, ((0, 32), (1, 16)))
    teacher_weight = gaussian(streams_of[1], (DT, DTO), DT ** -0.5, 0.046875, ((0, 16), (1, 32)))
    student_in = gaussian(streams_of[2], (TOKENS, DS), 1.0, 6.0, ((0, 32), (1, 16)))
    projection = gaussian(streams_of[3], (DS, DTO), DS ** -0.5, 0.0625, ((0, 16), (1, 32)))
    owner_order = draw_owner_order(jax.random.fold_in(streams_of[5], 71), 0)
    return dict(teacher_in=teacher_in, teacher_weight=teacher_weight, student_in=student_in, projection=projection, owner_order=owner_order)


def block_sum(left, right, nblocks):
    width = left.shape[1] // nblocks

    def add_block(kk, running):
        left_cols = lax.dynamic_slice_in_dim(left, (kk * width).astype(jnp.int32), width, 1)
        right_rows = lax.dynamic_slice_in_dim(right, (kk * width).astype(jnp.int32), width, 0)
        product = jnp.dot(left_cols, right_rows, preferred_element_type=jnp.float32)
        rounded = lax.optimization_barrier(product.astype(jnp.bfloat16))
        return running + rounded.astype(jnp.float32)
    start_sum = jnp.zeros((left.shape[0], right.shape[1]), jnp.float32)
    return lax.fori_loop(jnp.int32(0), jnp.int32(nblocks), add_block, start_sum)

def reference(teacher_in, teacher_weight, student_in, projection, owner_order):
    block_len = TOKENS // N_MP
    sub_len = block_len // N_MP
    teacher_out = block_sum(teacher_in, teacher_weight, N_MP).astype(jnp.bfloat16)
    positions = jnp.arange(TOKENS, dtype=jnp.int32)
    owner = positions // block_len
    within = positions % block_len
    source_block = within // sub_len
    inner_pos = within % sub_len
    source = source_block * block_len + owner_order[source_block * block_len + owner * sub_len + inner_pos]
    target = teacher_out[source].astype(jnp.float32)
    student_out = block_sum(student_in, projection, N_MP)
    inner = lax.optimization_barrier(jnp.sum(student_out * target, axis=1))
    sq_student = lax.optimization_barrier(jnp.sum(student_out * student_out, axis=1))
    sq_target = lax.optimization_barrier(jnp.sum(target * target, axis=1))
    inv_student = lax.rsqrt(sq_student + 1e-06)
    inv_target = lax.rsqrt(sq_target + 1e-06)
    cosine = inner * inv_student * inv_target
    scale = -1.0 / TOKENS
    grad_out = scale * (target * (inv_student * inv_target)[:, None] - (inner * inv_target * inv_student ** 3)[:, None] * student_out)
    grad_out = grad_out.astype(jnp.bfloat16)
    projection_grad = lax.dot_general(student_in, grad_out, (((0,), (0,)), ((), ())), preferred_element_type=jnp.float32)
    return (projection_grad, cosine)
```

```python
import jax
import jax.numpy as jnp
from jax import lax
from jax.sharding import Mesh, PartitionSpec as P

F32 = jnp.float32
BF16 = jnp.bfloat16
DP = ("z2", "z1", "z0", "x1", "x0")
MP = ("zh", "y", "c")


def spread(value, axis):
    count = lax.axis_size(axis)
    copies = jnp.broadcast_to(value[None], (count,) + value.shape)
    return lax.all_to_all(copies, axis, split_axis=0, concat_axis=0, tiled=True)


def reduce_over(value, axis):
    pieces = lax.all_to_all(value, axis, split_axis=0, concat_axis=0, tiled=True)
    return jnp.sum(pieces.astype(F32), axis=0)


def shards(teacher_in, teacher_weight, student_in, projection, owner_order):
    rows, teacher_width = teacher_in.shape
    student_width = student_in.shape[1]
    out_width = projection.shape[1]
    groups = 16
    block = owner_order.shape[0]
    sub = block // groups
    total_rows = groups * block

    orders = lax.all_gather(
        jnp.broadcast_to(owner_order[:, None], (block, block)), MP, axis=0, tiled=False
    )
    pick = (orders == lax.broadcasted_iota(jnp.int32, orders.shape, 2)).astype(BF16)

    both = jnp.concatenate([teacher_in, student_in], axis=1)
    for axis in ("z2", "z1", "z0", ("x1", "x0")):
        both = spread(both, axis)
    both = both.reshape(total_rows, teacher_width + student_width)
    teacher_all = both[:, :teacher_width]
    student_all = both[:, teacher_width:]

    teacher_part = jnp.dot(teacher_all, teacher_weight, preferred_element_type=F32).astype(BF16)
    student_part = jnp.dot(student_all, projection, preferred_element_type=F32).astype(BF16)

    def by_block(part):
        part = part.reshape(2, 2, 2, 2, 2, rows, out_width)
        return part.transpose(4, 3, 2, 0, 1, 5, 6).reshape(groups, block, out_width)

    teacher_rows = jnp.einsum(
        "bqk,bkn->bqn", pick, by_block(teacher_part), preferred_element_type=F32
    ).astype(BF16)
    teacher_rows = teacher_rows.reshape(groups, groups, sub, out_width)
    teacher_rows = teacher_rows.transpose(1, 0, 2, 3).reshape(groups, block, out_width)
    sums = jnp.stack([teacher_rows, by_block(student_part)])
    sums = sums.reshape(2, 2, 4, 2, block, out_width).transpose(3, 2, 1, 0, 4, 5)
    sums = reduce_over(sums, "c").astype(BF16)
    sums = reduce_over(sums, "y").astype(BF16)
    sums = reduce_over(sums, "zh")
    target = sums[0].astype(BF16).astype(F32)
    student_out = sums[1]

    stats = jnp.stack(
        [
            jnp.sum(student_out * target, axis=1),
            jnp.sum(student_out * student_out, axis=1),
            jnp.sum(target * target, axis=1),
        ]
    )
    stats = jnp.sum(spread(stats, ("x1", "x0")), axis=0)
    stats = jnp.sum(spread(stats, ("z2", "z1", "z0")), axis=0)
    inner, sq_student, sq_target = stats[0], stats[1], stats[2]
    inv_student = lax.rsqrt(sq_student + 1e-06)
    inv_target = lax.rsqrt(sq_target + 1e-06)
    cosine = inner * inv_student * inv_target
    scale = -1.0 / total_rows
    grad_out = scale * (
        target * (inv_student * inv_target)[:, None]
        - (inner * inv_target * inv_student**3)[:, None] * student_out
    )
    grad_out = grad_out.astype(BF16)
    for axis in ("zh", "y", "c"):
        grad_out = spread(grad_out, axis)
    grad_out = grad_out.reshape(2, 2, 2, 2, 2, rows, out_width)
    grad_out = grad_out.transpose(0, 4, 2, 1, 3, 5, 6).reshape(total_rows, out_width)
    projection_grad = lax.dot_general(
        student_all, grad_out, (((0,), (0,)), ((), ())), preferred_element_type=F32
    )
    return (projection_grad, cosine)


def solution(mesh):
    fine = Mesh(mesh.devices.reshape(2, 2, 2, 2, 2, 2, 4, 2), DP + MP)
    return jax.shard_map(
        shards,
        mesh=fine,
        in_specs=(P(DP, MP), P(MP, DP), P(DP, MP), P(MP, DP), P(MP)),
        out_specs=(P(MP, DP), P(MP)),
        check_vma=False,
    )
```

```python
import jax
import jax.numpy as jnp
from jax import lax
from jax.sharding import Mesh, PartitionSpec as P

F32 = jnp.float32
BF16 = jnp.bfloat16
DP = ("z2", "z1", "z0", "x")
MP = ("zh", "y1", "y0", "c")
SWAP = [(0, 1), (1, 0)]
UP = [(i, (i + 1) % 4) for i in range(4)]
DOWN = [(i, (i - 1) % 4) for i in range(4)]


def together(*values):
    return lax.optimization_barrier(values)


def swap_in(value, axis):
    other = lax.ppermute(value, axis, SWAP)
    first = lax.axis_index(axis) == 0
    both = jnp.stack([jnp.where(first, value, other), jnp.where(first, other, value)])
    return both.reshape((-1,) + value.shape[1:])


def spread(value, axis):
    count = lax.axis_size(axis)
    copies = jnp.broadcast_to(value[None], (count,) + value.shape)
    return lax.all_to_all(copies, axis, split_axis=0, concat_axis=0, tiled=True)


def neighbours(value):
    return lax.ppermute(value, "x", DOWN), lax.ppermute(value, "x", UP)


def opposite(after, before):
    half = after.shape[0] // 2
    return jnp.concatenate(
        [lax.ppermute(before[:half], "x", UP), lax.ppermute(after[half:], "x", DOWN)]
    )


def halve(value, axis):
    me = lax.axis_index(axis)
    other = lax.ppermute(
        lax.dynamic_index_in_dim(value, 1 - me, keepdims=False).astype(BF16), axis, SWAP
    )
    mine = lax.dynamic_index_in_dim(value, me, keepdims=False)
    return mine.astype(F32) + other.astype(F32)


def shards(teacher_in, teacher_weight, student_in, projection, owner_order):
    rows, teacher_width = teacher_in.shape
    out_width = projection.shape[1]
    groups = 16
    block = owner_order.shape[0]
    sub = block // groups
    total_rows = groups * block
    x = lax.axis_index("x")
    z0 = lax.axis_index("z0")
    part_width = teacher_width // 2

    def column_half(which):
        return lax.dynamic_slice_in_dim(teacher_in, which * part_width, part_width, 1)

    other = lax.ppermute(column_half(1 - z0), "z0", SWAP)
    mine = column_half(z0)
    orders = swap_in(owner_order[None], "c")
    other, orders = together(other, orders)
    teacher = jnp.concatenate([jnp.where(z0 == 0, mine, other), jnp.where(z0 == 0, other, mine)])
    teacher = swap_in(teacher, "z2")
    orders = swap_in(orders, "y0")
    teacher, orders = together(teacher, orders)
    teacher = swap_in(teacher, "z1")
    orders = swap_in(orders, "y1")

    teacher, student, orders, teacher_weight = together(
        teacher, student_in, orders, teacher_weight
    )
    after, before = neighbours(teacher)
    student = swap_in(student, "z2")
    orders = swap_in(orders, "zh")
    student = swap_in(student, "z1")
    weight_other = lax.ppermute(
        lax.dynamic_slice_in_dim(teacher_weight, (1 - z0) * part_width, part_width, 0), "z0", SWAP
    )
    weight_mine = lax.dynamic_slice_in_dim(teacher_weight, z0 * part_width, part_width, 0)
    after, before, student = together(after, before, student)
    far = opposite(after, before)
    teacher_blocks = (teacher, after, far, before)
    student = swap_in(student, "z0")
    student_after, student_before = neighbours(student)
    student_blocks = (student, student_after, opposite(student_after, student_before), student_before)

    pick = orders[:, :, None] == lax.broadcasted_iota(jnp.int32, (groups, block, block), 2)
    pick = pick.astype(BF16)

    def project(blocks, weight, order):
        width = weight.shape[1]
        part = jnp.zeros((4, total_rows // 4, width), BF16)
        for step, one in enumerate(blocks):
            product = jnp.dot(one, weight, preferred_element_type=F32).astype(BF16)
            part = lax.dynamic_update_slice_in_dim(part, product[None], (x + step) % 4, 0)
        part = part.reshape(2, 2, 2, 2, 2, rows, width)
        return part.transpose(order + (0, 1, 5, 6)).reshape(groups, block, width)

    def by_core(part):
        return part.reshape(2, 4, 2, block, -1).transpose(2, 1, 0, 3, 4)

    def reduced(part):
        part = lax.all_to_all(part, ("y1", "y0"), split_axis=0, concat_axis=0, tiled=True)
        part = jnp.sum(part.astype(F32), axis=0)
        other = lax.ppermute(part.astype(BF16), "zh", SWAP)
        return (part + other.astype(F32)).reshape(2 * block, out_width)

    weights = jnp.concatenate([weight_mine, weight_other], axis=1)
    teacher_rows = jnp.einsum(
        "bqk,bkn->bqn",
        pick,
        project(teacher_blocks, weights, (3, 2, 4)),
        preferred_element_type=F32,
    ).astype(BF16)
    teacher_rows = teacher_rows.reshape(groups, groups, sub, 2 * out_width)
    teacher_rows = teacher_rows.transpose(1, 0, 2, 3).reshape(groups, block, 2 * out_width)
    teacher_rows = halve(by_core(teacher_rows), "c")
    arrived = lax.ppermute(teacher_rows[..., out_width:].astype(BF16), "z0", SWAP)
    teacher_rows = teacher_rows[..., :out_width] + arrived.astype(F32)
    target = reduced(teacher_rows.astype(BF16)).astype(BF16).astype(F32)

    student_rows = by_core(project(student_blocks, projection, (4, 3, 2)))
    student_out = reduced(halve(student_rows, "c").astype(BF16))

    stats = jnp.stack(
        [
            jnp.sum(student_out * target, axis=1),
            jnp.sum(student_out * student_out, axis=1),
            jnp.sum(target * target, axis=1),
        ]
    )
    stats = jnp.sum(spread(stats, "x"), axis=0)
    stats = jnp.sum(spread(stats, ("z2", "z1", "z0")), axis=0)
    inner, sq_student, sq_target = stats[0], stats[1], stats[2]
    inv_student = lax.rsqrt(sq_student + 1e-06)
    inv_target = lax.rsqrt(sq_target + 1e-06)
    cosine = inner * inv_student * inv_target
    scale = -1.0 / total_rows
    grad_out = scale * (
        target * (inv_student * inv_target)[:, None]
        - (inner * inv_target * inv_student**3)[:, None] * student_out
    )
    grad_out = grad_out.astype(BF16)
    cosine = lax.dynamic_slice_in_dim(cosine, lax.axis_index("zh") * block, block)
    grad_out = spread(grad_out, ("y1", "y0"))
    grad_out = swap_in(grad_out[None], "c")
    grad_out = grad_out.reshape(2, 2, 2, 2, 2, rows, out_width)
    grad_out = grad_out.transpose(0, 4, 2, 1, 3, 5, 6).reshape(4, total_rows // 4, out_width)
    projection_grad = 0.0
    for step, one in enumerate(student_blocks):
        projection_grad += lax.dot_general(
            one,
            lax.dynamic_index_in_dim(grad_out, (x + step) % 4, keepdims=False),
            (((0,), (0,)), ((), ())),
            preferred_element_type=F32,
        )
    return (projection_grad, cosine)


def solution(mesh):
    fine = Mesh(mesh.devices.reshape(2, 2, 2, 4, 2, 2, 2, 2), DP + MP)
    return jax.shard_map(
        shards,
        mesh=fine,
        in_specs=(P(DP, MP), P(MP, DP), P(DP, MP), P(MP, DP), P(MP)),
        out_specs=(P(MP, DP), P(MP)),
        check_vma=False,
    )
```

```python
import jax
import jax.numpy as jnp
from jax import lax
from jax.sharding import Mesh, PartitionSpec as P

F32 = jnp.float32
BF16 = jnp.bfloat16
YC = ("y1", "y0", "c")
DP = ("z2", "z1", "z0", "x")
MP = ("zh", "y1", "y0", "c")
SWAP = [(0, 1), (1, 0)]


def together(*values):
    return lax.optimization_barrier(values)


def in_order(value, other, axis):
    first = lax.axis_index(axis) == 0
    both = jnp.stack([jnp.where(first, value, other), jnp.where(first, other, value)])
    return both.reshape((-1,) + value.shape[1:])


def swap_in(value, axis):
    return in_order(value, lax.ppermute(value, axis, SWAP), axis)


def spread(value, axis):
    count = lax.axis_size(axis)
    copies = jnp.broadcast_to(value[None], (count,) + value.shape)
    return lax.all_to_all(copies, axis, split_axis=0, concat_axis=0, tiled=True)


def summed(pieces, axis):
    part = lax.all_to_all(pieces, axis, split_axis=0, concat_axis=0, tiled=True)
    return jnp.sum(part.astype(F32), axis=0)


def halve(value, axis):
    me = lax.axis_index(axis)
    other = lax.dynamic_index_in_dim(value, 1 - me, keepdims=False)
    other = lax.ppermute(other.astype(BF16), axis, SWAP)
    return lax.dynamic_index_in_dim(value, me, keepdims=False).astype(F32) + other.astype(F32)


def both_owners(part):
    other = lax.ppermute(part.astype(BF16), "zh", SWAP)
    return (part + other.astype(F32)).reshape(-1, part.shape[-1])


def shards(teacher_in, teacher_weight, student_in, projection, owner_order):
    rows, out_width = teacher_in.shape[0], projection.shape[1]
    groups = 16
    block = owner_order.shape[0]
    sub = block // groups
    total_rows = groups * block
    core = lax.axis_index("c")
    z0 = lax.axis_index("z0")
    part_width = teacher_in.shape[1] // 4
    student_width = student_in.shape[1]

    quarters = jnp.concatenate(
        [
            teacher_in.reshape(rows, 4, part_width).transpose(1, 0, 2),
            teacher_weight.reshape(4, part_width, out_width),
        ],
        axis=1,
    )
    quarters = lax.all_to_all(quarters, "x", split_axis=0, concat_axis=0, tiled=True)
    student, quarters = together(swap_in(student_in, "z2"), quarters)
    teacher = quarters[:, :rows].reshape(4 * rows, part_width)
    weights = quarters[:, rows:]
    student, teacher, orders = together(
        swap_in(student, "z1"), swap_in(teacher, "z2"), spread(owner_order, YC)
    )
    student, teacher, orders = together(swap_in(student, "z0"), swap_in(teacher, "z1"), orders)
    student_all, teacher, orders = together(
        spread(student, "x"), swap_in(teacher, "z0"), swap_in(orders, "zh")
    )
    student_all = student_all.reshape(total_rows, student_width)
    student_part = jnp.dot(student_all, projection, preferred_element_type=F32).astype(BF16)
    student_part = student_part.reshape(2, 2, 2, 2, 2, rows, out_width)
    student_part = student_part.transpose(3, 2, 0, 4, 1, 5, 6).reshape(8, 2, block, out_width)
    student_part, teacher = together(student_part, teacher)
    student_part = summed(student_part, YC)
    pick = orders[:, :, None] == lax.broadcasted_iota(jnp.int32, (groups, block, block), 2)
    pick = pick.astype(BF16)

    teacher = teacher.reshape(2, 2, 2, 2, 2, rows, part_width)
    teacher = teacher.transpose(2, 1, 0, 3, 4, 5, 6).reshape(groups, block, part_width)
    teacher = jnp.einsum("bqk,bkn->bqn", pick, teacher, preferred_element_type=F32).astype(BF16)
    teacher = teacher.reshape(groups, 2, 4, 2, sub, part_width)
    teacher = teacher.transpose(3, 2, 1, 0, 4, 5).reshape(2, total_rows // 2, part_width)

    def product(which):
        one = lax.dynamic_index_in_dim(teacher, which, keepdims=False)
        return [
            jnp.dot(one, weights[place], preferred_element_type=F32).astype(BF16)
            for place in range(4)
        ]

    arrived = lax.ppermute(jnp.stack(product(1 - core)), "c", SWAP)
    own = together(*product(core))
    part = jnp.stack(
        [(own[place].astype(F32) + arrived[place].astype(F32)).astype(BF16) for place in range(4)]
    )
    part = part.reshape(16, 2, block, out_width)
    part, student_part = together(part, student_part)
    part = summed(part, ("x", "y1", "y0"))
    student_out = both_owners(student_part)
    part, student_out = together(part, student_out)
    target = both_owners(part).astype(BF16)
    target = target.astype(F32)

    stats = jnp.stack(
        [
            jnp.sum(student_out * target, axis=1),
            jnp.sum(student_out * student_out, axis=1),
            jnp.sum(target * target, axis=1),
        ]
    )
    stats = jnp.sum(spread(stats, "x"), axis=0)
    stats = jnp.sum(spread(stats, ("z2", "z1", "z0")), axis=0)
    inner, sq_student, sq_target = stats[0], stats[1], stats[2]
    inv_student = lax.rsqrt(sq_student + 1e-06)
    inv_target = lax.rsqrt(sq_target + 1e-06)
    cosine = inner * inv_student * inv_target
    scale = -1.0 / total_rows
    grad_out = scale * (
        target * (inv_student * inv_target)[:, None]
        - (inner * inv_target * inv_student**3)[:, None] * student_out
    )
    grad_out = grad_out.astype(BF16)
    cosine = lax.dynamic_slice_in_dim(cosine, lax.axis_index("zh") * block, block)
    grad_out = spread(grad_out, ("y1", "y0"))
    grad_out = swap_in(grad_out[None], "c")
    grad_out = grad_out.reshape(2, 2, 2, 2, 2, rows, out_width)
    grad_out = grad_out.transpose(0, 4, 2, 1, 3, 5, 6).reshape(total_rows, out_width)
    projection_grad = lax.dot_general(
        student_all, grad_out, (((0,), (0,)), ((), ())), preferred_element_type=F32
    )
    return (projection_grad, cosine)


def solution(mesh):
    fine = Mesh(mesh.devices.reshape(2, 2, 2, 4, 2, 2, 2, 2), DP + MP)
    return jax.shard_map(
        shards,
        mesh=fine,
        in_specs=(P(DP, MP), P(MP, DP), P(DP, MP), P(MP, DP), P(MP)),
        out_specs=(P(MP, DP), P(MP)),
        check_vma=False,
    )
```

```python
import jax
import jax.numpy as jnp
from jax import lax
from jax.sharding import Mesh, PartitionSpec as P

F32 = jnp.float32
BF16 = jnp.bfloat16
YC = ("y1", "y0", "c")
DP = ("z2", "z1", "z0", "x")
MP = ("zh", "y1", "y0", "c")
SWAP = [(0, 1), (1, 0)]


def together(*values):
    return lax.optimization_barrier(values)


def in_order(value, other, axis):
    first = lax.axis_index(axis) == 0
    both = jnp.stack([jnp.where(first, value, other), jnp.where(first, other, value)])
    return both.reshape((-1,) + value.shape[1:])


def swap_in(value, axis):
    return in_order(value, lax.ppermute(value, axis, SWAP), axis)


def spread(value, axis):
    count = lax.axis_size(axis)
    copies = jnp.broadcast_to(value[None], (count,) + value.shape)
    return lax.all_to_all(copies, axis, split_axis=0, concat_axis=0, tiled=True)


def summed(pieces, axis):
    part = lax.all_to_all(pieces, axis, split_axis=0, concat_axis=0, tiled=True)
    return jnp.sum(part.astype(F32), axis=0)


def halve(value, axis):
    me = lax.axis_index(axis)
    other = lax.dynamic_index_in_dim(value, 1 - me, keepdims=False)
    other = lax.ppermute(other.astype(BF16), axis, SWAP)
    return lax.dynamic_index_in_dim(value, me, keepdims=False).astype(F32) + other.astype(F32)


def both_owners(part):
    other = lax.ppermute(part.astype(BF16), "zh", SWAP)
    return (part + other.astype(F32)).reshape(-1, part.shape[-1])


def shards(teacher_in, teacher_weight, student_in, projection, owner_order):
    rows, out_width = teacher_in.shape[0], projection.shape[1]
    groups = 16
    block = owner_order.shape[0]
    sub = block // groups
    total_rows = groups * block
    core = lax.axis_index("c")
    z0 = lax.axis_index("z0")
    part_width = teacher_in.shape[1] // 4
    student_width = student_in.shape[1]

    quarters = jnp.concatenate(
        [
            teacher_in.reshape(rows, 4, part_width).transpose(1, 0, 2),
            teacher_weight.reshape(4, part_width, out_width),
        ],
        axis=1,
    )
    quarters = lax.all_to_all(quarters, "x", split_axis=0, concat_axis=0, tiled=True)
    student, quarters = together(swap_in(student_in, "z2"), quarters)
    teacher = quarters[:, :rows].reshape(4 * rows, part_width)
    weights = quarters[:, rows:]
    student, teacher, orders = together(
        swap_in(student, "z1"), swap_in(teacher, "z2"), owner_order
    )
    student, orders = together(swap_in(student, "z0"), spread(orders, YC))
    student_all, teacher, orders = together(
        spread(student, "x"), swap_in(swap_in(teacher, "z1"), "z0"), swap_in(orders, "zh")
    )
    student_all = student_all.reshape(total_rows, student_width)
    student_part = jnp.dot(student_all, projection, preferred_element_type=F32).astype(BF16)
    student_part = student_part.reshape(2, 2, 2, 2, 2, rows, out_width)
    student_part = student_part.transpose(3, 2, 0, 4, 1, 5, 6).reshape(8, 2, block, out_width)
    student_part, teacher = together(student_part, teacher)
    student_part = lax.all_to_all(student_part, YC, split_axis=0, concat_axis=0, tiled=True)
    pick = orders[:, :, None] == lax.broadcasted_iota(jnp.int32, (groups, block, block), 2)
    pick = pick.astype(BF16)

    teacher = teacher.reshape(2, 2, 2, 2, 2, rows, part_width)
    teacher = teacher.transpose(2, 1, 0, 3, 4, 5, 6).reshape(groups, block, part_width)
    teacher = jnp.einsum("bqk,bkn->bqn", pick, teacher, preferred_element_type=F32).astype(BF16)
    teacher = teacher.reshape(groups, 2, 4, 2, sub, part_width)
    teacher = teacher.transpose(3, 2, 1, 0, 4, 5).reshape(2, total_rows // 2, part_width)

    def product(which):
        one = lax.dynamic_index_in_dim(teacher, which, keepdims=False)
        return [
            jnp.dot(one, weights[place], preferred_element_type=F32).astype(BF16)
            for place in range(4)
        ]

    arrived = lax.ppermute(jnp.stack(product(1 - core)), "c", SWAP)
    own = together(*product(core))
    part = jnp.stack(
        [(own[place].astype(F32) + arrived[place].astype(F32)).astype(BF16) for place in range(4)]
    )
    part = part.reshape(16, 2, block, out_width)
    part, student_part = together(part, student_part)
    part = summed(part, ("x", "y1", "y0"))
    student_out = both_owners(jnp.sum(student_part.astype(F32), axis=0))
    part, student_out = together(part, student_out)
    target = both_owners(part).astype(BF16)
    target = target.astype(F32)

    stats = jnp.stack(
        [
            jnp.sum(student_out * target, axis=1),
            jnp.sum(student_out * student_out, axis=1),
            jnp.sum(target * target, axis=1),
        ]
    )
    stats = jnp.sum(spread(stats, "x"), axis=0)
    stats = jnp.sum(spread(stats, ("z2", "z1", "z0")), axis=0)
    inner, sq_student, sq_target = stats[0], stats[1], stats[2]
    inv_student = lax.rsqrt(sq_student + 1e-06)
    inv_target = lax.rsqrt(sq_target + 1e-06)
    cosine = inner * inv_student * inv_target
    scale = -1.0 / total_rows
    grad_out = scale * (
        target * (inv_student * inv_target)[:, None]
        - (inner * inv_target * inv_student**3)[:, None] * student_out
    )
    grad_out = grad_out.astype(BF16)
    cosine = lax.dynamic_slice_in_dim(cosine, lax.axis_index("zh") * block, block)
    grad_out = spread(grad_out, ("y1", "y0"))
    grad_out = swap_in(grad_out[None], "c")
    grad_out = grad_out.reshape(2, 2, 2, 2, 2, rows, out_width)
    grad_out = grad_out.transpose(0, 4, 2, 1, 3, 5, 6).reshape(total_rows, out_width)
    projection_grad = lax.dot_general(
        student_all, grad_out, (((0,), (0,)), ((), ())), preferred_element_type=F32
    )
    return (projection_grad, cosine)


def solution(mesh):
    fine = Mesh(mesh.devices.reshape(2, 2, 2, 4, 2, 2, 2, 2), DP + MP)
    return jax.shard_map(
        shards,
        mesh=fine,
        in_specs=(P(DP, MP), P(MP, DP), P(DP, MP), P(MP, DP), P(MP)),
        out_specs=(P(MP, DP), P(MP)),
        check_vma=False,
    )
```

```python
import jax
import jax.numpy as jnp
from jax import lax
from jax.sharding import Mesh, PartitionSpec as P

F32 = jnp.float32
BF16 = jnp.bfloat16
YC = ("y1", "y0", "c")
DP = ("z2", "z1", "z0", "x")
MP = ("zh", "y1", "y0", "c")
SWAP = [(0, 1), (1, 0)]


def together(*values):
    return lax.optimization_barrier(values)


def in_order(value, other, axis):
    first = lax.axis_index(axis) == 0
    both = jnp.stack([jnp.where(first, value, other), jnp.where(first, other, value)])
    return both.reshape((-1,) + value.shape[1:])


def swap_in(value, axis):
    return in_order(value, lax.ppermute(value, axis, SWAP), axis)


def spread(value, axis):
    count = lax.axis_size(axis)
    copies = jnp.broadcast_to(value[None], (count,) + value.shape)
    return lax.all_to_all(copies, axis, split_axis=0, concat_axis=0, tiled=True)


def summed(pieces, axis):
    part = lax.all_to_all(pieces, axis, split_axis=0, concat_axis=0, tiled=True)
    return jnp.sum(part.astype(F32), axis=0)


def halve(value, axis):
    me = lax.axis_index(axis)
    other = lax.dynamic_index_in_dim(value, 1 - me, keepdims=False)
    other = lax.ppermute(other.astype(BF16), axis, SWAP)
    return lax.dynamic_index_in_dim(value, me, keepdims=False).astype(F32) + other.astype(F32)


def both_owners(part):
    other = lax.ppermute(part.astype(BF16), "zh", SWAP)
    return (part + other.astype(F32)).reshape(-1, part.shape[-1])


def shards(teacher_in, teacher_weight, student_in, projection, owner_order):
    rows, out_width = teacher_in.shape[0], projection.shape[1]
    groups = 16
    block = owner_order.shape[0]
    sub = block // groups
    total_rows = groups * block
    core = lax.axis_index("c")
    z0 = lax.axis_index("z0")
    part_width = teacher_in.shape[1] // 4
    student_width = student_in.shape[1]

    quarters = jnp.concatenate(
        [
            teacher_in.reshape(rows, 4, part_width).transpose(1, 0, 2),
            teacher_weight.reshape(4, part_width, out_width),
        ],
        axis=1,
    )
    quarters = lax.all_to_all(quarters, "x", split_axis=0, concat_axis=0, tiled=True)
    student, quarters = together(swap_in(student_in, "z2"), quarters)
    teacher = quarters[:, :rows].reshape(4 * rows, part_width)
    weights = quarters[:, rows:]
    student, teacher, orders = together(
        swap_in(student, "z1"), swap_in(teacher, "z2"), owner_order
    )
    student, orders = together(swap_in(student, "z0"), spread(orders, YC))
    student_all, teacher, orders = together(
        spread(student, "x"), swap_in(swap_in(teacher, "z1"), "z0"), swap_in(orders, "zh")
    )
    student_all = student_all.reshape(total_rows, student_width)
    student_part = jnp.dot(student_all, projection, preferred_element_type=F32).astype(BF16)
    student_part = student_part.reshape(2, 2, 2, 2, 2, rows, out_width)
    student_part = student_part.transpose(3, 2, 0, 4, 1, 5, 6).reshape(8, 2, block, out_width)
    student_part, teacher = together(student_part, teacher)
    student_part = lax.all_to_all(student_part, YC, split_axis=0, concat_axis=0, tiled=True)
    pick = orders[:, :, None] == lax.broadcasted_iota(jnp.int32, (groups, block, block), 2)
    pick = pick.astype(BF16)

    teacher = teacher.reshape(2, 2, 2, 2, 2, rows, part_width)
    teacher = teacher.transpose(2, 1, 0, 3, 4, 5, 6).reshape(groups, block, part_width)
    teacher = jnp.einsum("bqk,bkn->bqn", pick, teacher, preferred_element_type=F32).astype(BF16)
    teacher = teacher.reshape(groups, 2, 4, 2, sub, part_width)
    teacher = teacher.transpose(3, 2, 1, 0, 4, 5).reshape(2, total_rows // 2, part_width)

    def product(which):
        one = lax.dynamic_index_in_dim(teacher, which, keepdims=False)
        return [
            jnp.dot(one, weights[place], preferred_element_type=F32).astype(BF16)
            for place in range(4)
        ]

    arrived = lax.ppermute(jnp.stack(product(1 - core)), "c", SWAP)
    own = together(*product(core))
    part = jnp.stack(
        [(own[place].astype(F32) + arrived[place].astype(F32)).astype(BF16) for place in range(4)]
    )
    part = part.reshape(16, 2, block, out_width)
    part, student_part = together(part, student_part)
    part = summed(part, ("x", "y1", "y0"))
    student_out = both_owners(jnp.sum(student_part.astype(F32), axis=0))
    part, student_out = together(part, student_out)
    target = both_owners(part).astype(BF16)
    target = target.astype(F32)

    stats = jnp.stack(
        [
            jnp.sum(student_out * target, axis=1),
            jnp.sum(student_out * student_out, axis=1),
            jnp.sum(target * target, axis=1),
        ]
    )
    stats = jnp.sum(spread(stats, DP), axis=0)
    inner, sq_student, sq_target = stats[0], stats[1], stats[2]
    inv_student = lax.rsqrt(sq_student + 1e-06)
    inv_target = lax.rsqrt(sq_target + 1e-06)
    cosine = inner * inv_student * inv_target
    scale = -1.0 / total_rows
    grad_out = scale * (
        target * (inv_student * inv_target)[:, None]
        - (inner * inv_target * inv_student**3)[:, None] * student_out
    )
    grad_out = grad_out.astype(BF16)
    cosine = lax.dynamic_slice_in_dim(cosine, lax.axis_index("zh") * block, block)
    grad_out = spread(grad_out, ("y1", "y0"))
    grad_out = swap_in(grad_out[None], "c")
    grad_out = grad_out.reshape(2, 2, 2, 2, 2, rows, out_width)
    grad_out = grad_out.transpose(0, 4, 2, 1, 3, 5, 6).reshape(total_rows, out_width)
    projection_grad = lax.dot_general(
        student_all, grad_out, (((0,), (0,)), ((), ())), preferred_element_type=F32
    )
    return (projection_grad, cosine)


def solution(mesh):
    fine = Mesh(mesh.devices.reshape(2, 2, 2, 4, 2, 2, 2, 2), DP + MP)
    return jax.shard_map(
        shards,
        mesh=fine,
        in_specs=(P(DP, MP), P(MP, DP), P(DP, MP), P(MP, DP), P(MP)),
        out_specs=(P(MP, DP), P(MP)),
        check_vma=False,
    )
```

```python
import jax
import jax.numpy as jnp
from jax import lax
from jax.sharding import Mesh, PartitionSpec as P

F32 = jnp.float32
BF16 = jnp.bfloat16
YC = ("y1", "y0", "c")
DP = ("z2", "z1", "z0", "x")
MP = ("zh", "y1", "y0", "c")
SWAP = [(0, 1), (1, 0)]


def together(*values):
    return lax.optimization_barrier(values)


def in_order(value, other, axis):
    first = lax.axis_index(axis) == 0
    both = jnp.stack([jnp.where(first, value, other), jnp.where(first, other, value)])
    return both.reshape((-1,) + value.shape[1:])


def swap_in(value, axis):
    return in_order(value, lax.ppermute(value, axis, SWAP), axis)


def spread(value, axis):
    count = lax.axis_size(axis)
    copies = jnp.broadcast_to(value[None], (count,) + value.shape)
    return lax.all_to_all(copies, axis, split_axis=0, concat_axis=0, tiled=True)


def summed(pieces, axis):
    part = lax.all_to_all(pieces, axis, split_axis=0, concat_axis=0, tiled=True)
    return jnp.sum(part.astype(F32), axis=0)


def halve(value, axis):
    me = lax.axis_index(axis)
    other = lax.dynamic_index_in_dim(value, 1 - me, keepdims=False)
    other = lax.ppermute(other.astype(BF16), axis, SWAP)
    return lax.dynamic_index_in_dim(value, me, keepdims=False).astype(F32) + other.astype(F32)


def both_owners(part):
    other = lax.ppermute(part.astype(BF16), "zh", SWAP)
    return (part + other.astype(F32)).reshape(-1, part.shape[-1])


def shards(teacher_in, teacher_weight, student_in, projection, owner_order):
    rows, out_width = teacher_in.shape[0], projection.shape[1]
    groups = 16
    block = owner_order.shape[0]
    sub = block // groups
    total_rows = groups * block
    core = lax.axis_index("c")
    z0 = lax.axis_index("z0")
    part_width = teacher_in.shape[1] // 4
    student_width = student_in.shape[1]

    quarters = jnp.concatenate(
        [
            teacher_in.reshape(rows, 4, part_width).transpose(1, 0, 2),
            teacher_weight.reshape(4, part_width, out_width),
        ],
        axis=1,
    )
    quarters = lax.all_to_all(quarters, "x", split_axis=0, concat_axis=0, tiled=True)
    student, quarters = together(swap_in(student_in, "z2"), quarters)
    teacher = quarters[:, :rows].reshape(4 * rows, part_width)
    weights = quarters[:, rows:]
    student, teacher, orders = together(
        swap_in(student, "z1"), swap_in(teacher, "z2"), owner_order
    )
    student, orders = together(swap_in(student, "z0"), spread(orders, YC))
    student_all, teacher, orders = together(
        spread(student, "x"), swap_in(swap_in(teacher, "z1"), "z0"), swap_in(orders, "zh")
    )
    student_all = student_all.reshape(total_rows, student_width)
    student_part = jnp.dot(student_all, projection, preferred_element_type=F32).astype(BF16)
    student_part = student_part.reshape(2, 2, 2, 2, 2, rows, out_width)
    student_part = student_part.transpose(3, 2, 0, 4, 1, 5, 6).reshape(8, 2, block, out_width)
    student_part, teacher = together(student_part, teacher)
    student_part = lax.all_to_all(student_part, YC, split_axis=0, concat_axis=0, tiled=True)
    pick = orders[:, :, None] == lax.broadcasted_iota(jnp.int32, (groups, block, block), 2)
    pick = pick.astype(BF16)

    teacher = teacher.reshape(2, 2, 2, 2, 2, rows, part_width)
    teacher = teacher.transpose(2, 1, 0, 3, 4, 5, 6).reshape(groups, block, part_width)
    teacher = jnp.einsum("bqk,bkn->bqn", pick, teacher, preferred_element_type=F32).astype(BF16)
    teacher = teacher.reshape(groups, 2, 4, 2, sub, part_width)
    teacher = teacher.transpose(3, 2, 1, 0, 4, 5).reshape(2, total_rows // 2, part_width)

    def product(which):
        one = lax.dynamic_index_in_dim(teacher, which, keepdims=False)
        return [
            jnp.dot(one, weights[place], preferred_element_type=F32).astype(BF16)
            for place in range(4)
        ]

    arrived = lax.ppermute(jnp.stack(product(1 - core)), "c", SWAP)
    own = together(*product(core))
    part = jnp.stack(
        [(own[place].astype(F32) + arrived[place].astype(F32)).astype(BF16) for place in range(4)]
    )
    part = part.reshape(16, 2, block, out_width)
    part, student_part = together(part, student_part)
    part = summed(part, ("x", "y1", "y0"))
    student_out = both_owners(jnp.sum(student_part.astype(F32), axis=0))
    part, student_out = together(part, student_out)
    target = both_owners(part).astype(BF16)
    target = target.astype(F32)

    stats = jnp.stack(
        [
            jnp.sum(student_out * target, axis=1),
            jnp.sum(student_out * student_out, axis=1),
            jnp.sum(target * target, axis=1),
        ]
    )
    stats = jnp.sum(spread(stats, DP), axis=0)
    inner, sq_student, sq_target = stats[0], stats[1], stats[2]
    inv_student = lax.rsqrt(sq_student + 1e-06)
    inv_target = lax.rsqrt(sq_target + 1e-06)
    cosine = inner * inv_student * inv_target
    scale = -1.0 / total_rows
    grad_out = scale * (
        target * (inv_student * inv_target)[:, None]
        - (inner * inv_target * inv_student**3)[:, None] * student_out
    )
    grad_out = grad_out.astype(BF16)
    cosine = lax.dynamic_slice_in_dim(cosine, lax.axis_index("zh") * block, block)
    grad_out = spread(grad_out, YC)
    grad_out = grad_out.reshape(2, 2, 2, 2, 2, rows, out_width)
    grad_out = grad_out.transpose(2, 4, 1, 0, 3, 5, 6).reshape(total_rows, out_width)
    projection_grad = lax.dot_general(
        student_all, grad_out, (((0,), (0,)), ((), ())), preferred_element_type=F32
    )
    return (projection_grad, cosine)


def solution(mesh):
    fine = Mesh(mesh.devices.reshape(2, 2, 2, 4, 2, 2, 2, 2), DP + MP)
    return jax.shard_map(
        shards,
        mesh=fine,
        in_specs=(P(DP, MP), P(MP, DP), P(DP, MP), P(MP, DP), P(MP)),
        out_specs=(P(MP, DP), P(MP)),
        check_vma=False,
    )
```

```python
import jax
import jax.numpy as jnp
from jax import lax
from jax.sharding import Mesh, PartitionSpec as P

F32 = jnp.float32
BF16 = jnp.bfloat16
YC = ("y1", "y0", "c")
DP = ("z2", "z1", "z0", "x")
MP = ("zh", "y1", "y0", "c")
SWAP = [(0, 1), (1, 0)]


def together(*values):
    return lax.optimization_barrier(values)


def in_order(value, other, axis):
    first = lax.axis_index(axis) == 0
    both = jnp.stack([jnp.where(first, value, other), jnp.where(first, other, value)])
    return both.reshape((-1,) + value.shape[1:])


def swap_in(value, axis):
    return in_order(value, lax.ppermute(value, axis, SWAP), axis)


def spread(value, axis):
    count = lax.axis_size(axis)
    copies = jnp.broadcast_to(value[None], (count,) + value.shape)
    return lax.all_to_all(copies, axis, split_axis=0, concat_axis=0, tiled=True)


def summed(pieces, axis):
    part = lax.all_to_all(pieces, axis, split_axis=0, concat_axis=0, tiled=True)
    return jnp.sum(part.astype(F32), axis=0)


def halve(value, axis):
    me = lax.axis_index(axis)
    other = lax.dynamic_index_in_dim(value, 1 - me, keepdims=False)
    other = lax.ppermute(other.astype(BF16), axis, SWAP)
    return lax.dynamic_index_in_dim(value, me, keepdims=False).astype(F32) + other.astype(F32)


def both_owners(part):
    other = lax.ppermute(part.astype(BF16), "zh", SWAP)
    return (part + other.astype(F32)).reshape(-1, part.shape[-1])


def shards(teacher_in, teacher_weight, student_in, projection, owner_order):
    rows, out_width = teacher_in.shape[0], projection.shape[1]
    groups = 16
    block = owner_order.shape[0]
    sub = block // groups
    total_rows = groups * block
    core = lax.axis_index("c")
    z0 = lax.axis_index("z0")
    part_width = teacher_in.shape[1] // 4
    student_width = student_in.shape[1]

    quarters = jnp.concatenate(
        [
            teacher_in.reshape(rows, 4, part_width).transpose(1, 0, 2),
            teacher_weight.reshape(4, part_width, out_width),
        ],
        axis=1,
    )
    quarters = lax.all_to_all(quarters, "x", split_axis=0, concat_axis=0, tiled=True)
    student, quarters = together(swap_in(student_in, "z2"), quarters)
    teacher = quarters[:, :rows].reshape(4 * rows, part_width)
    weights = quarters[:, rows:]
    student, teacher, orders = together(
        swap_in(student, "z1"), swap_in(teacher, "z2"), swap_in(owner_order[None], "zh")
    )
    student, orders = together(swap_in(student, "z0"), spread(orders, YC))
    student_all, teacher, orders = together(
        spread(student, "x"), swap_in(swap_in(teacher, "z1"), "z0"), orders
    )
    orders = orders.transpose(1, 0, 2).reshape(groups, block)
    student_all = student_all.reshape(total_rows, student_width)
    student_part = jnp.dot(student_all, projection, preferred_element_type=F32).astype(BF16)
    student_part = student_part.reshape(2, 2, 2, 2, 2, rows, out_width)
    student_part = student_part.transpose(3, 2, 0, 4, 1, 5, 6).reshape(8, 2, block, out_width)
    student_part, teacher = together(student_part, teacher)
    student_part = lax.all_to_all(student_part, YC, split_axis=0, concat_axis=0, tiled=True)
    pick = orders[:, :, None] == lax.broadcasted_iota(jnp.int32, (groups, block, block), 2)
    pick = pick.astype(BF16)

    teacher = teacher.reshape(2, 2, 2, 2, 2, rows, part_width)
    teacher = teacher.transpose(2, 1, 0, 3, 4, 5, 6).reshape(groups, block, part_width)
    teacher = jnp.einsum("bqk,bkn->bqn", pick, teacher, preferred_element_type=F32).astype(BF16)
    teacher = teacher.reshape(groups, 2, 4, 2, sub, part_width)
    teacher = teacher.transpose(3, 2, 1, 0, 4, 5).reshape(2, total_rows // 2, part_width)

    def product(which):
        one = lax.dynamic_index_in_dim(teacher, which, keepdims=False)
        return [
            jnp.dot(one, weights[place], preferred_element_type=F32).astype(BF16)
            for place in range(4)
        ]

    arrived = lax.ppermute(jnp.stack(product(1 - core)), "c", SWAP)
    own = together(*product(core))
    part = jnp.stack(
        [(own[place].astype(F32) + arrived[place].astype(F32)).astype(BF16) for place in range(4)]
    )
    part = part.reshape(16, 2, block, out_width)
    part, student_part = together(part, student_part)
    part = summed(part, ("x", "y1", "y0"))
    student_out = both_owners(jnp.sum(student_part.astype(F32), axis=0))
    part, student_out = together(part, student_out)
    target = both_owners(part).astype(BF16)
    target = target.astype(F32)

    stats = jnp.stack(
        [
            jnp.sum(student_out * target, axis=1),
            jnp.sum(student_out * student_out, axis=1),
            jnp.sum(target * target, axis=1),
        ]
    )
    stats = jnp.sum(spread(stats, DP), axis=0)
    inner, sq_student, sq_target = stats[0], stats[1], stats[2]
    inv_student = lax.rsqrt(sq_student + 1e-06)
    inv_target = lax.rsqrt(sq_target + 1e-06)
    cosine = inner * inv_student * inv_target
    scale = -1.0 / total_rows
    grad_out = scale * (
        target * (inv_student * inv_target)[:, None]
        - (inner * inv_target * inv_student**3)[:, None] * student_out
    )
    grad_out = grad_out.astype(BF16)
    cosine = lax.dynamic_slice_in_dim(cosine, lax.axis_index("zh") * block, block)
    grad_out = spread(grad_out, ("y1", "y0"))
    grad_out = swap_in(grad_out[None], "c")
    grad_out = grad_out.reshape(2, 2, 2, 2, 2, rows, out_width)
    grad_out = grad_out.transpose(0, 4, 2, 1, 3, 5, 6).reshape(total_rows, out_width)
    projection_grad = lax.dot_general(
        student_all, grad_out, (((0,), (0,)), ((), ())), preferred_element_type=F32
    )
    return (projection_grad, cosine)


def solution(mesh):
    fine = Mesh(mesh.devices.reshape(2, 2, 2, 4, 2, 2, 2, 2), DP + MP)
    return jax.shard_map(
        shards,
        mesh=fine,
        in_specs=(P(DP, MP), P(MP, DP), P(DP, MP), P(MP, DP), P(MP)),
        out_specs=(P(MP, DP), P(MP)),
        check_vma=False,
    )
```
